32 devices in a mesh: gx: 4 (over z), gy: 2 (over y), gz: 4 (over x, core).
Axes of the slice: x: 2, y: 2, z: 4, core: 2. Of those that a mesh axis runs over, the one named last changes fastest.
Arguments:
- offsets: float32 [3, 8, 4, 8, 128], P(None, 'gx', 'gy', 'gz'), may hold values from 0 to 1
- features: bfloat16 [16, 8, 4, 8, 128], P(None, 'gx', 'gy', 'gz'), may hold values from -6 to 6
- charges: float32 [8, 8, 4, 8, 128], P(None, 'gx', 'gy', 'gz'), may hold values from -3 to 3
- counts: int32 [8, 4, 8], P('gx', 'gy', 'gz'), may hold values from 64 to 128, as said below
- waves: int32 [3, 2048], replicated, may hold values from -8 to 8, as said below
- kernel: float32 [8, 2048], replicated, may hold values from 0.1 to 3
- w_feat: float32 [16, 16], replicated, may hold values from -1.5 to 1.5
- w_charge_h: float32 [16, 8], replicated, may hold values from -1.5 to 1.5
- w_charge_f: float32 [8, 8], replicated, may hold values from -2 to 2
- charge_bias: float32 [8], replicated, may hold values from -1 to 1
- w_move_h: float32 [16, 3], replicated, may hold values from -1.5 to 1.5
- w_move_f: float32 [8, 3], replicated, may hold values from -2 to 2
Outputs:
- new_offsets: float32 [3, 8, 4, 8, 128], P(None, 'gx', 'gy', 'gz')
- new_charges: float32 [8, 8, 4, 8, 128], P(None, 'gx', 'gy', 'gz')
- new_features: bfloat16 [16, 8, 4, 8, 128], P(None, 'gx', 'gy', 'gz')
- last_field: float32 [8, 8, 4, 8, 128], P(None, 'gx', 'gy', 'gz')
The draws below stay inside these ranges and needn't reach their ends.
Inputs may be any that keep to these rules, and one draw needn't show every extreme that they name: `counts`: live atoms of each cell; slots from the count on are empty and their entries are ignored. `waves`: the first component of every wavevector is from 1 to 8.
All inputs are finite; a program needn't handle non-finite values.
Results may differ from the reference program's by a relative error of at most 0.0042.
Values may be sent and summed in bfloat16 or wider, within the bound.
A program may use at most 64 MiB of HBM per device.

```python
import math
import jax
import jax.numpy as jnp
from jax import lax

CAP = 128
FEAT = 16
CHG = 8
K = 2048
KMAX = 8
STEPS = 2
ITERS = 2
NX = 8
NY = 4
NZ = 8
ATOMS = 32768


def draw_counts(key, part):
    drawn_counts = jax.random.randint(key, (NX * NY * NZ,), CAP // 2, CAP + 1)
    position_index = jnp.arange(NX * NY * NZ, dtype=jnp.int32)
    drawn_counts = jnp.where(position_index == 0, CAP, drawn_counts)
    drawn_counts = jnp.where(position_index == NX * NY * NZ - 1, CAP // 2, drawn_counts)
    return drawn_counts.reshape(NX, NY, NZ).astype(jnp.int32)


def draw_waves(key, part):
    first_key, second_key = jax.random.split(key)
    leading = jax.random.randint(first_key, (1, K), 1, KMAX + 1)
    others = jax.random.randint(second_key, (2, K), -KMAX, KMAX + 1)
    stacked = jnp.concatenate([leading, others], axis=0)
    column_index = jnp.arange(K, dtype=jnp.int32)[None, :]
    extreme = jnp.array([[KMAX], [-KMAX], [KMAX]], dtype=jnp.int32)
    return jnp.where(column_index == 0, extreme, stacked).astype(jnp.int32)


def block_scale(key, shape, shards, least, largest):
    gain = 1.0
    for dim, blocks in shards:
        heights = jax.random.uniform(jax.random.fold_in(jax.random.fold_in(key, 6), dim), (blocks,), jnp.float32, least / len(shards), largest / len(shards))
        gain = gain * jnp.repeat(jnp.exp(heights), shape[dim] // blocks).reshape((-1,) + (1,) * (len(shape) - 1 - dim))
    return gain


def scatter_about(rng, extent, scale, limit, cuts=(), held_as=jnp.bfloat16):
    factor_of = block_scale(rng, extent, cuts, -0.22, 0.18) if cuts else 1.0
    values = jax.random.normal(rng, extent, jnp.float32) * scale * factor_of
    return jnp.minimum(jnp.maximum(values, -limit), limit).astype(held_as)


def setup_inputs(seed: int = 0) -> dict:
    key_list = jax.random.split(jax.random.key(seed), 13)
    return {
        "offsets": jnp.clip(1.0 * jax.random.uniform(key_list[0], (3, NX, NY, NZ, CAP), jnp.float32) ** block_scale(key_list[0], (3, NX, NY, NZ, CAP), ((1, 4), (2, 2), (3, 4)), -0.2, 0.2), 0.0, 1.0),
        "features": scatter_about(key_list[1], (FEAT, NX, NY, NZ, CAP), 1.0, 6.0, ((1, 4), (2, 2), (3, 4))),
        "charges": scatter_about(key_list[2], (CHG, NX, NY, NZ, CAP), 0.5, 3.0, ((1, 4), (2, 2), (3, 4)), jnp.float32),
        "counts": draw_counts(jax.random.fold_in(key_list[12], 71), 0),
        "waves": draw_waves(jax.random.fold_in(key_list[12], 71), 0),
        "kernel": jnp.clip(jnp.exp(jax.random.uniform(key_list[5], (CHG, K), jnp.float32, math.log(0.1), math.log(3.0))), 0.1, 3.0),
        "w_feat": scatter_about(key_list[6], (FEAT, FEAT), FEAT ** -0.5, 1.5, (), jnp.float32),
        "w_charge_h": scatter_about(key_list[7], (FEAT, CHG), FEAT ** -0.5, 1.5, (), jnp.float32),
        "w_charge_f": scatter_about(key_list[8], (CHG, CHG), CHG ** -0.5, 2.0, (), jnp.float32),
        "charge_bias": jnp.clip(jax.random.uniform(key_list[9], (CHG,), jnp.float32, -1.0, 1.0), -1.0, 1.0),
        "w_move_h": scatter_about(key_list[10], (FEAT, 3), FEAT ** -0.5, 1.5, (), jnp.float32),
        "w_move_f": scatter_about(key_list[11], (CHG, 3), CHG ** -0.5, 2.0, (), jnp.float32),
    }


RC_COEF = 1.0 / 0.72
STEP_LEN = 0.1
TWO_PI = 2.0 * math.pi
PRECISE = lax.Precision.HIGHEST

def phase_table(frac_rows, wave_float):
    theta = TWO_PI * (wave_float[0][None, :] * frac_rows[0][:, None] + wave_float[1][None, :] * frac_rows[1][:, None] + wave_float[2][None, :] * frac_rows[2][:, None])
    return jnp.concatenate([jnp.cos(theta), jnp.sin(theta)], axis=1)

def pair_messages(positions, feats, valid_slot):
    message = jnp.zeros(feats.shape, jnp.float32)
    norm_sum = jnp.zeros(valid_slot.shape, jnp.float32)
    for shift_x in (-1, 0, 1):
        for shift_y in (-1, 0, 1):
            for shift_z in (-1, 0, 1):
                moves = (-shift_x, -shift_y, -shift_z)
                near_pos = jnp.roll(positions, moves, axis=(1, 2, 3))
                near_feat = jnp.roll(feats, moves, axis=(1, 2, 3))
                near_valid = jnp.roll(valid_slot, moves, axis=(0, 1, 2))
                dist_x = near_pos[0][..., None, :] - positions[0][..., :, None] + shift_x
                dist_y = near_pos[1][..., None, :] - positions[1][..., :, None] + shift_y
                dist_z = near_pos[2][..., None, :] - positions[2][..., :, None] + shift_z
                dist_sq = dist_x * dist_x + dist_y * dist_y + dist_z * dist_z
                weight = (valid_slot[..., :, None] * near_valid[..., None, :] * jnp.exp(-dist_sq * RC_COEF)).astype(jnp.bfloat16)
                weight_wide = weight.astype(jnp.float32)
                message = message + jnp.einsum('xyzab,cxyzb->cxyza', weight_wide, near_feat.astype(jnp.float32))
                norm_sum = norm_sum + lax.optimization_barrier(jnp.sum(weight_wide, axis=-1))
    return message / jnp.sqrt(jnp.maximum(norm_sum, 1.0))

def to_cells(grid_array):
    return grid_array.reshape(grid_array.shape[0], NX * NY * NZ, CAP).transpose(1, 0, 2)

def from_cells(cell_array):
    return cell_array.transpose(1, 0, 2).reshape(cell_array.shape[1], NX, NY, NZ, CAP)

def fractions(positions):
    cell_x = jnp.arange(NX, dtype=jnp.int32).astype(jnp.float32)
    cell_y = jnp.arange(NY, dtype=jnp.int32).astype(jnp.float32)
    cell_z = jnp.arange(NZ, dtype=jnp.int32).astype(jnp.float32)
    frac_x = (cell_x[:, None, None, None] + positions[0]) / NX
    frac_y = (cell_y[None, :, None, None] + positions[1]) / NY
    frac_z = (cell_z[None, None, :, None] + positions[2]) / NZ
    return to_cells(jnp.stack([frac_x, frac_y, frac_z]))

def structure_all(frac_cells, charge_rows, wave_float):

    def per_cell(running, item_pair):
        return (running + jnp.dot(item_pair[1], phase_table(item_pair[0], wave_float), precision=PRECISE), None)
    start = jnp.zeros((charge_rows.shape[1], 2 * wave_float.shape[1]), jnp.float32)
    summed, _ = lax.scan(per_cell, start, (frac_cells, charge_rows))
    return summed

def field_all(frac_cells, weighted, wave_float, scale):

    def per_cell(frac_rows):
        return jnp.dot(weighted, phase_table(frac_rows, wave_float).T, precision=PRECISE) * scale
    return lax.map(per_cell, frac_cells)

def reference(offsets, features, charges, counts, waves, kernel, w_feat, w_charge_h, w_charge_f, charge_bias, w_move_h, w_move_f):
    scale = 1.0 / math.sqrt(ATOMS * K)
    wave_float = waves.astype(jnp.float32)
    doubled = jnp.concatenate([kernel, kernel], axis=1)
    valid_slot = (jnp.arange(CAP, dtype=jnp.int32)[None, None, None, :] < counts[..., None]).astype(jnp.float32)
    valid_cells = valid_slot.reshape(NX * NY * NZ, CAP)
    positions = offsets
    feats = features
    charge_cells = to_cells(charges * valid_slot[None])
    field_cells = jnp.zeros_like(charge_cells)
    for step_index in range(STEPS):
        message = pair_messages(positions, feats, valid_slot)
        feats = (feats.astype(jnp.float32) + jnp.tanh(jnp.einsum('fg,fxyzp->gxyzp', w_feat, message, precision=PRECISE))).astype(jnp.bfloat16)
        frac_cells = fractions(positions)
        hproj = jnp.einsum('fc,nfp->ncp', w_charge_h, to_cells(feats.astype(jnp.float32)), precision=PRECISE)
        for sweep in range(ITERS):
            totals = lax.optimization_barrier(jnp.sum(charge_cells, axis=(0, 2)))
            atom_count = jnp.sum(valid_cells)
            average = totals / atom_count
            neutral = valid_cells[:, None, :] * (charge_cells - average[None, :, None])
            summed = structure_all(frac_cells, neutral, wave_float)
            field_cells = field_all(frac_cells, doubled * summed, wave_float, scale)
            fproj = jnp.einsum('dc,ndp->ncp', w_charge_f, field_cells, precision=PRECISE)
            charge_cells = valid_cells[:, None, :] * (0.5 * neutral + jnp.tanh(hproj + fproj + charge_bias[None, :, None]))
        field_grid = from_cells(field_cells)
        move = jnp.tanh(jnp.einsum('fd,fxyzp->dxyzp', w_move_h, message, precision=PRECISE) + jnp.einsum('cd,cxyzp->dxyzp', w_move_f, field_grid, precision=PRECISE))
        positions = positions + STEP_LEN * valid_slot * move
    return (positions, from_cells(charge_cells), feats, from_cells(field_cells))
```

```python
import functools
import math

import jax
import jax.numpy as jnp
import numpy as np
from jax import lax
from jax.experimental import pallas as pl
from jax.experimental.pallas import tpu as pltpu
from jax.sharding import PartitionSpec as P

STEPS = 2
ITERS = 2
STEP_LEN = 0.1
CAP = 128
EXP_COEF = math.log2(math.e) / 0.72
FAR = 1.0e6
HI = lax.Precision.HIGHEST
MESH = pl.DeviceIdType.MESH
REC = 32
N_P = 37
TILES_PV = 5
TOT = 37
PV0 = 38
TILES = PV0 + TILES_PV


def fit(fn):
    cheb = np.polynomial.chebyshev.Chebyshev.interpolate(fn, 8, domain=[0.0, 0.25])
    return [float(v) for v in cheb.convert(kind=np.polynomial.Polynomial).coef]


COS_POLY = fit(lambda s: np.cos(2 * np.pi * np.sqrt(np.abs(s))))
SIN_POLY = fit(lambda s: 2 * np.pi * np.sinc(2 * np.sqrt(np.abs(s))))


def horner(coefs, x):
    total = jnp.full_like(x, coefs[-1])
    for c in reversed(coefs[:-1]):
        total = total * x + c
    return total


def split3(x):
    hi = x.astype(jnp.bfloat16)
    rest = x - hi.astype(jnp.float32)
    mid = rest.astype(jnp.bfloat16)
    low = (rest - mid.astype(jnp.float32)).astype(jnp.bfloat16)
    return hi, mid, low


def split2(x):
    hi = x.astype(jnp.bfloat16)
    return hi, (x - hi.astype(jnp.float32)).astype(jnp.bfloat16)


def dot(a, b, dims, precision=None):
    return lax.dot_general(
        a, b, (dims, ((), ())), precision=precision, preferred_element_type=jnp.float32
    )


def dot3(a, b, dims):
    ah, al = split2(a)
    bh, bl = split2(b)
    return dot(ah, bh, dims) + (dot(ah, bl, dims) + dot(al, bh, dims))


NN = ((1,), (0,))
NT = ((1,), (1,))
TN = ((0,), (0,))


def spans(size, d):
    if d == 0:
        return 1, 1, size
    if d > 0:
        return size, 0, 1
    return 1, size + 1, 1


def kernel_body(
    sizes, block, chunk,
    pos_in, feat_in, charge_in, valid_in, waves_ref, kern_ref, wfeat_ref, wch_ref, wcf_ref,
    bias_ref, wmh_ref, wmf_ref,
    pos_out, charge_out, feat_out, field_out,
    halo, bt_ref, a_ref, msg_ref, yz_ref, w_ref, payload, rs_buf, part_buf, gx_buf, full,
    halo_send, halo_recv, rs_send, rs_recv, gx_send, gx_recv, ag_send, ag_recv,
):
    nx, ny, nz = sizes
    sx, sy, sz = block
    atoms = sx * sy * sz * CAP
    plane = ny * nz
    mx, my, mz = lax.axis_index("gx"), lax.axis_index("gy"), lax.axis_index("gz")
    mp = my * nz + mz
    scale = 1.0 / math.sqrt(nx * sx * ny * sy * nz * sz * CAP * waves_ref.shape[1])

    def plane_id(d):
        p = lax.rem(mp + d, plane)
        return (mx, lax.div(p, nz), lax.rem(p, nz)), p

    barrier = pltpu.get_barrier_semaphore()
    for ddx in range(nx):
        for d in range(plane):
            if ddx == 0 and d == 0:
                continue
            (_, py, pz), _ = plane_id(d)
            pl.semaphore_signal(
                barrier, inc=1, device_id=(lax.rem(mx + ddx, nx), py, pz), device_id_type=MESH
            )

    valid = valid_in[...]
    cell = lax.broadcasted_iota(jnp.int32, (1, atoms), 1) // CAP
    loc = [cell // (sy * sz), (cell // sz) % sy, cell % sz]
    mine = [mx, my, mz]
    side = [nx * sx, ny * sy, nz * sz]
    cell_f = [
        (loc[j] + mine[j] * block[j]).astype(jnp.float32) for j in range(3)
    ]
    local_f = jnp.concatenate([v.astype(jnp.float32) for v in loc], axis=0) - 1.0
    lane = lax.broadcasted_iota(jnp.int32, (8, 128), 1)
    sub = lax.broadcasted_iota(jnp.int32, (8, 128), 0)
    k8 = (lax.broadcasted_iota(jnp.int32, (8, 1), 0) + 1).astype(jnp.float32)

    wy, wz = waves_ref[1:2, :], waves_ref[2:3, :]
    sgy = jnp.where(wy > 0, 1.0, 0.0) - jnp.where(wy < 0, 1.0, 0.0)
    sgz = jnp.where(wz > 0, 1.0, 0.0) - jnp.where(wz < 0, 1.0, 0.0)
    k8i = lax.broadcasted_iota(jnp.int32, (8, 1), 0) + 1
    oz = (jnp.abs(wz) == k8i).astype(jnp.float32)
    oy = (jnp.abs(wy) == k8i).astype(jnp.float32)
    oz0 = (wz == 0).astype(jnp.float32)
    oy0 = (wy == 0).astype(jnp.float32)
    hot = [oy[i : i + 1] * oz for i in range(8)] + [oy0 * oz, oy * oz0, oy0 * oz0 * (k8 == 1.0)]
    kern = kern_ref[...]
    lanes_k = [jnp.where(waves_ref[0:1, :] == i + 1, kern, 0.0) for i in range(8)]
    lanes_k = jnp.concatenate(lanes_k + lanes_k, axis=0)
    kh, kl = split2(lanes_k)
    sx_lane = jnp.where(lane >= 64, 1.0, -1.0)
    hot = jnp.concatenate(hot, axis=0)
    for i, sg in enumerate((None, sgy * sgz, sgy, sgz)):
        oh = (hot if sg is None else hot * sg).astype(jnp.bfloat16)
        w = (dot(oh, kh, NT) + dot(oh, kl, NT)) * scale
        if i >= 2:
            w = w * sx_lane[0:1]
        w_ref[i] = w

    pl.semaphore_wait(barrier, nx * plane - 1)

    def send_halo(step, pos, feats):
        hi, mid, low = split3(pos)
        rec = jnp.concatenate(
            [feats.astype(jnp.float32)]
            + [v.astype(jnp.float32) for v in (hi, mid, low)]
            + [valid, jnp.zeros((REC - 26, atoms), jnp.float32)],
            axis=0,
        ).astype(jnp.bfloat16)
        for x in range(sx):
            for y in range(sy):
                for z in range(sz):
                    n = (x * sy + y) * sz + z
                    halo[step, 1 + x, 1 + y, 1 + z] = rec[:, n * CAP : (n + 1) * CAP]
        copies = []
        for dx in (-1, 0, 1):
            for dy in (-1, 0, 1):
                for dz in (-1, 0, 1):
                    if dx == dy == dz == 0:
                        continue
                    n = len(copies)
                    x, y, z = spans(sx, dx), spans(sy, dy), spans(sz, dz)
                    copy = pltpu.make_async_remote_copy(
                        src_ref=halo.at[
                            step, pl.ds(x[0], x[2]), pl.ds(y[0], y[2]), pl.ds(z[0], z[2])
                        ],
                        dst_ref=halo.at[
                            step, pl.ds(x[1], x[2]), pl.ds(y[1], y[2]), pl.ds(z[1], z[2])
                        ],
                        send_sem=halo_send.at[step, n],
                        recv_sem=halo_recv.at[step, n],
                        device_id=(
                            lax.rem(mx + nx + dx, nx),
                            lax.rem(my + ny + dy, ny),
                            lax.rem(mz + nz + dz, nz),
                        ),
                        device_id_type=MESH,
                    )
                    copy.start()
                    copies.append(copy)
        return copies

    def pair_rows(p, ok, own):
        width = p.shape[1]
        sq = -EXP_COEF * (p[0:1] * p[0:1] + p[1:2] * p[1:2] + p[2:3] * p[2:3])
        one = jnp.ones((3, width), jnp.float32)
        f32 = lambda parts: [v.astype(jnp.float32) for v in parts]
        if own:
            hi, mid, low = f32(split3(p * (2.0 * EXP_COEF)))
            rows = [hi, mid, low, hi, mid, hi, one] + f32(split3(sq))
        else:
            hi, mid, low = f32(split3(p))
            rows = [hi, hi, hi, mid, mid, low] + f32(split3(sq - FAR * (1.0 - ok))) + [one]
        return jnp.concatenate(rows + [jnp.zeros((8, width), jnp.float32)], axis=0)

    def pair_messages(step, pos):
        own = pair_rows(pos + local_f, None, True).astype(jnp.bfloat16)
        for i in range(sx * sy):
            a_ref[i] = own[:, i * sz * CAP : (i + 1) * sz * CAP]
        wide = (sz + 2) * CAP
        zrow = (lax.broadcasted_iota(jnp.int32, (1, wide), 1) // CAP).astype(jnp.float32) - 2.0

        def prepare(g, carry):
            gx_i, gy_i = lax.div(g, sy + 2), lax.rem(g, sy + 2)
            rec = jnp.concatenate(
                [halo[step, gx_i, gy_i, z] for z in range(sz + 2)], axis=1
            ).astype(jnp.float32)
            p = rec[16:19] + rec[19:22] + rec[22:25]
            ones = jnp.ones((1, wide), jnp.float32)
            base = jnp.concatenate(
                [
                    ones * (gx_i.astype(jnp.float32) - 2.0),
                    ones * (gy_i.astype(jnp.float32) - 2.0),
                    zrow,
                ],
                axis=0,
            )
            bt_ref[g] = jnp.transpose(pair_rows(p + base, rec[25:26], False)).astype(jnp.bfloat16)
            return carry

        lax.fori_loop(0, (sx + 2) * (sy + 2), prepare, 0)

        def per_column(i, carry):
            x, y = lax.div(i, sy), lax.rem(i, sy)
            for z in range(sz):
                mine_a = a_ref[i, :, z * CAP : (z + 1) * CAP]
                total = jnp.zeros((REC, CAP), jnp.float32)
                for dx in range(3):
                    for dy in range(3):
                        g = (x + dx) * (sy + 2) + y + dy
                        rows = bt_ref[g, z * CAP : (z + 3) * CAP, :]
                        weight = jnp.exp2(dot(rows, mine_a, NN)).astype(jnp.bfloat16)
                        rec = jnp.concatenate(
                            [halo[step, x + dx, y + dy, z + k] for k in range(3)], axis=1
                        )
                        total = total + dot(rec, weight, NN)
                msg_ref[i, :, z * CAP : (z + 1) * CAP] = total
            return carry

        lax.fori_loop(0, sx * sy, per_column, 0)
        total = jnp.concatenate([msg_ref[i] for i in range(sx * sy)], axis=1) * valid
        return total[0:16] / jnp.sqrt(jnp.maximum(total[25:26], 1.0))

    def all_sum(r):
        copies = []
        for d in range(1, plane):
            device, p = plane_id(d)
            copy = pltpu.make_async_remote_copy(
                src_ref=payload.at[r, pl.ds(pl.multiple_of(p * chunk, 8), chunk)],
                dst_ref=rs_buf.at[r, d],
                send_sem=rs_send.at[r, d],
                recv_sem=rs_recv.at[r, d],
                device_id=device,
                device_id_type=MESH,
            )
            copy.start()
            copies.append(copy)
        total = payload[r, pl.ds(pl.multiple_of(mp * chunk, 8), chunk)]
        for d in range(1, plane):
            copies[d - 1].wait_recv()
            total = total + rs_buf[r, d]
        part_buf[r, 0] = total
        copies_x = []
        for d in range(1, nx):
            copy = pltpu.make_async_remote_copy(
                src_ref=part_buf.at[r, 0],
                dst_ref=gx_buf.at[r, d],
                send_sem=gx_send.at[r, d],
                recv_sem=gx_recv.at[r, d],
                device_id=(lax.rem(mx + d, nx), my, mz),
                device_id_type=MESH,
            )
            copy.start()
            copies_x.append(copy)
        for d in range(1, nx):
            copies_x[d - 1].wait_recv()
            total = total + gx_buf[r, d]
        here = pl.ds(pl.multiple_of(mp * chunk, 8), chunk)
        full[r, here] = total
        copies_g = []
        for d in range(1, plane):
            device, _ = plane_id(d)
            copy = pltpu.make_async_remote_copy(
                src_ref=full.at[r, here],
                dst_ref=full.at[r, here],
                send_sem=ag_send.at[r, d],
                recv_sem=ag_recv.at[r, d],
                device_id=device,
                device_id_type=MESH,
            )
            copy.start()
            copies_g.append(copy)
        for copy in copies_g:
            copy.wait_recv()
        for copy in copies + copies_x + copies_g:
            copy.wait_send()

    def trig(pos):
        out = []
        for j in range(3):
            u = (cell_f[j] + pos[j : j + 1]) / float(side[j])
            t = k8 * u
            t = t - jnp.floor(t + 0.5)
            s = t * t
            out.append((horner(COS_POLY, s), t * horner(SIN_POLY, s)))
        return out

    block_ones = (
        lax.broadcasted_iota(jnp.int32, (128, 128), 0) // 8
        == lax.broadcasted_iota(jnp.int32, (128, 128), 1) // 8
    ).astype(jnp.bfloat16)

    pos = pos_in[...]
    feats = feat_in[...]
    charge = charge_in[...] * valid
    field = None
    count_row = jnp.zeros((1, 128), jnp.float32) + jnp.sum(valid, axis=1, keepdims=True)
    ones8 = jnp.ones((8, atoms), jnp.bfloat16)
    for step in range(STEPS):
        copies = send_halo(step, pos, feats)
        (cx, sxn), (cy, syn), (cz, szn) = trig(pos)
        xs = [v[i : i + 1] for v in (cx, sxn) for i in range(8)]
        zz = jnp.concatenate([cz, szn], axis=0)
        for i in range(16):
            yrow = (cy, syn)[i // 8][i % 8 : i % 8 + 1]
            yz_ref[i * 16 : (i + 1) * 16, :] = yrow * zz
        yz_ref[256:272, :] = zz
        yz_ref[272:288, :] = jnp.concatenate([cy, syn], axis=0)
        yz_ref[288:296, :] = jnp.where(k8 == 1.0, 1.0, 0.0) * jnp.ones((8, atoms), jnp.float32)
        yz = yz_ref[...]
        yh, yl = split2(yz)
        valid8 = jnp.ones((8, 1), jnp.float32) * valid
        xv = jnp.concatenate([x * valid8 for x in xs], axis=0)
        vh, vl = split2(xv)
        pv = dot(yh, vh, NT) + (dot(yh, vl, NT) + dot(yl, vh, NT))
        for t in range(TILES_PV):
            packed = jnp.zeros((8, 128), jnp.float32)
            for g in range(8):
                if t * 8 + g < N_P:
                    n = t * 8 + g
                    packed = jnp.where(lane % 8 == g, pv[n * 8 : n * 8 + 8], packed)
            payload[step * ITERS, (PV0 + t) * 8 : (PV0 + t + 1) * 8] = packed
        for copy in copies:
            copy.wait()
        message = pair_messages(step, pos)
        feats = (
            feats.astype(jnp.float32)
            + jnp.tanh(dot(wfeat_ref[...], message, TN, HI))
        ).astype(jnp.bfloat16)
        hproj = dot(wch_ref[...], feats.astype(jnp.float32), TN, HI) + bias_ref[...]
        for sweep in range(ITERS):
            r = step * ITERS + sweep
            qx = jnp.concatenate([x * charge for x in xs], axis=0)
            qh, ql = split2(qx)
            payload[r, 0 : N_P * 8] = dot(yh, qh, NT) + (dot(yh, ql, NT) + dot(yl, qh, NT))
            qrep = jnp.concatenate([charge] * 16, axis=0)
            th, tm, tl = split3(qrep)
            totals = dot(ones8, th, NT) + dot(ones8, tm, NT) + dot(ones8, tl, NT)
            payload[r, TOT * 8 : TOT * 8 + 8] = jnp.where(sub == 0, totals, count_row)
            if sweep > 0:
                payload[r, PV0 * 8 : TILES * 8] = jnp.zeros((TILES_PV * 8, 128), jnp.float32)
            if payload.shape[1] > TILES * 8:
                payload[r, TILES * 8 :] = jnp.zeros(
                    (payload.shape[1] - TILES * 8, 128), jnp.float32
                )
            all_sum(r)
            if sweep == 0:
                spread = []
                for n in range(N_P):
                    packed = full[r, (PV0 + n // 8) * 8 : (PV0 + n // 8) * 8 + 8]
                    spread.append(jnp.where(lane % 8 == n % 8, packed, 0.0))
                sh, sm, sl = split3(jnp.concatenate(spread, axis=0))
                pv_all = dot(sh, block_ones, NN) + dot(sm, block_ones, NN) + dot(sl, block_ones, NN)
            tot = full[r, TOT * 8 : TOT * 8 + 8]
            mean_row = tot[0:1] / tot[1:2]
            mean_col = jnp.sum(
                jnp.where(lane == sub, jnp.broadcast_to(mean_row, (8, 128)), 0.0),
                axis=1, keepdims=True,
            )
            neutral = valid * (charge - mean_col)
            p_all = full[r, 0 : N_P * 8] - mean_row * pv_all
            p_roll = pltpu.roll(p_all, 64, 1)
            tile = lambda a, n: a[n * 8 : n * 8 + 8]
            t_rows = []
            for yr in range(2):
                for ky in range(8):
                    for zr in range(2):
                        w = [w_ref[i, ky * 8 : ky * 8 + 8] for i in range(4)]
                        at = lambda a, b: ((a * 8 + ky) * 2 + b)
                        s_y, s_z = 2.0 * yr - 1.0, 2.0 * zr - 1.0
                        t_rows.append(
                            w[0] * tile(p_all, at(yr, zr))
                            - (s_y * s_z) * w[1] * tile(p_all, at(1 - yr, 1 - zr))
                            - s_y * w[2] * tile(p_roll, at(1 - yr, zr))
                            - s_z * w[3] * tile(p_roll, at(yr, 1 - zr))
                        )
            for zr in range(2):
                t_rows.append(
                    w_ref[0, 64:72] * tile(p_all, 32 + zr)
                    - (2.0 * zr - 1.0) * w_ref[3, 64:72] * tile(p_roll, 32 + 1 - zr)
                )
            for yr in range(2):
                t_rows.append(
                    w_ref[0, 72:80] * tile(p_all, 34 + yr)
                    - (2.0 * yr - 1.0) * w_ref[2, 72:80] * tile(p_roll, 34 + 1 - yr)
                )
            t_rows.append(w_ref[0, 80:88] * tile(p_all, 36))
            t_all = jnp.transpose(jnp.concatenate(t_rows, axis=0))
            fh, fl = split2(t_all)
            f_all = dot(fh, yh, NN) + (dot(fh, yl, NN) + dot(fl, yh, NN))
            field = xs[0] * f_all[0:8]
            for i in range(1, 16):
                field = field + xs[i] * f_all[i * 8 : i * 8 + 8]
            fproj = dot(wcf_ref[...], field, TN, HI)
            charge = valid * (0.5 * neutral + jnp.tanh(hproj + fproj))
        move = jnp.tanh(
            dot(wmh_ref[...], message, TN, HI) + dot(wmf_ref[...], field, TN, HI)
        )
        pos = pos + STEP_LEN * valid * move
    pos_out[...] = pos
    charge_out[...] = charge
    feat_out[...] = feats
    field_out[...] = field


def on_device(
    sizes, offsets, features, charges, counts, waves, kernel,
    w_feat, w_charge_h, w_charge_f, charge_bias, w_move_h, w_move_f,
):
    nx, ny, nz = sizes
    block = offsets.shape[1:4]
    sx, sy, sz = block
    atoms = sx * sy * sz * CAP
    plane = ny * nz
    chunk = -(-TILES // plane) * 8
    rounds = STEPS * ITERS
    valid = (jnp.arange(CAP, dtype=jnp.int32) < counts[..., None]).astype(jnp.float32)
    args = (
        offsets.reshape(3, atoms), features.reshape(16, atoms), charges.reshape(8, atoms),
        valid.reshape(1, atoms), waves, kernel, w_feat, w_charge_h, w_charge_f,
        charge_bias.reshape(8, 1), w_move_h, w_move_f,
    )
    vmem = pl.BlockSpec(memory_space=pltpu.VMEM)
    dma = pltpu.SemaphoreType.DMA
    outs = pl.pallas_call(
        functools.partial(kernel_body, sizes, block, chunk),
        out_shape=(
            jax.ShapeDtypeStruct((3, atoms), jnp.float32),
            jax.ShapeDtypeStruct((8, atoms), jnp.float32),
            jax.ShapeDtypeStruct((16, atoms), jnp.bfloat16),
            jax.ShapeDtypeStruct((8, atoms), jnp.float32),
        ),
        in_specs=[vmem] * len(args),
        out_specs=(vmem,) * 4,
        scratch_shapes=[
            pltpu.VMEM((STEPS, sx + 2, sy + 2, sz + 2, REC, CAP), jnp.bfloat16),
            pltpu.VMEM(((sx + 2) * (sy + 2), (sz + 2) * CAP, 32), jnp.bfloat16),
            pltpu.VMEM((sx * sy, 32, sz * CAP), jnp.bfloat16),
            pltpu.VMEM((sx * sy, REC, sz * CAP), jnp.float32),
            pltpu.VMEM((N_P * 8, atoms), jnp.float32),
            pltpu.VMEM((4, 88, 128), jnp.float32),
            pltpu.VMEM((rounds, plane * chunk, 128), jnp.float32),
            pltpu.VMEM((rounds, plane, chunk, 128), jnp.float32),
            pltpu.VMEM((rounds, 1, chunk, 128), jnp.float32),
            pltpu.VMEM((rounds, nx, chunk, 128), jnp.float32),
            pltpu.VMEM((rounds, plane * chunk, 128), jnp.float32),
            dma((STEPS, 26)), dma((STEPS, 26)),
            dma((rounds, plane)), dma((rounds, plane)),
            dma((rounds, nx)), dma((rounds, nx)),
            dma((rounds, plane)), dma((rounds, plane)),
        ],
        compiler_params=pltpu.CompilerParams(
            collective_id=0, has_side_effects=True, vmem_limit_bytes=48 * 1024 * 1024
        ),
    )(*args)
    return (
        outs[0].reshape(offsets.shape), outs[1].reshape(charges.shape),
        outs[2].reshape(features.shape), outs[3].reshape(charges.shape),
    )


def solution(mesh):
    grid = P(None, "gx", "gy", "gz", None)
    sizes = tuple(mesh.shape[a] for a in ("gx", "gy", "gz"))
    return jax.shard_map(
        functools.partial(on_device, sizes),
        mesh=mesh,
        in_specs=(grid, grid, grid, P("gx", "gy", "gz")) + (P(),) * 8,
        out_specs=(grid,) * 4,
        check_vma=False,
    )
```

```python
import functools
import math

import jax
import jax.numpy as jnp
import numpy as np
from jax import lax
from jax.experimental import pallas as pl
from jax.experimental.pallas import tpu as pltpu
from jax.sharding import PartitionSpec as P

STEPS = 2
ITERS = 2
STEP_LEN = 0.1
CAP = 128
EXP_COEF = math.log2(math.e) / 0.72
FAR = 1.0e6
HI = lax.Precision.HIGHEST
MESH = pl.DeviceIdType.MESH
REC = 32
N_P = 37
TILES_PV = 5
TOT = 37
PV0 = 38
TILES = PV0 + TILES_PV


def fit(fn):
    cheb = np.polynomial.chebyshev.Chebyshev.interpolate(fn, 8, domain=[0.0, 0.25])
    return [float(v) for v in cheb.convert(kind=np.polynomial.Polynomial).coef]


COS_POLY = fit(lambda s: np.cos(2 * np.pi * np.sqrt(np.abs(s))))
SIN_POLY = fit(lambda s: 2 * np.pi * np.sinc(2 * np.sqrt(np.abs(s))))


def horner(coefs, x):
    total = jnp.full_like(x, coefs[-1])
    for c in reversed(coefs[:-1]):
        total = total * x + c
    return total


def split3(x):
    hi = x.astype(jnp.bfloat16)
    rest = x - hi.astype(jnp.float32)
    mid = rest.astype(jnp.bfloat16)
    low = (rest - mid.astype(jnp.float32)).astype(jnp.bfloat16)
    return hi, mid, low


def split2(x):
    hi = x.astype(jnp.bfloat16)
    return hi, (x - hi.astype(jnp.float32)).astype(jnp.bfloat16)


def dot(a, b, dims, precision=None):
    return lax.dot_general(
        a, b, (dims, ((), ())), precision=precision, preferred_element_type=jnp.float32
    )


def dot3(a, b, dims):
    ah, al = split2(a)
    bh, bl = split2(b)
    return dot(ah, bh, dims) + (dot(ah, bl, dims) + dot(al, bh, dims))


NN = ((1,), (0,))
NT = ((1,), (1,))
TN = ((0,), (0,))


def spans(size, d):
    if d == 0:
        return 1, 1, size
    if d > 0:
        return size, 0, 1
    return 1, size + 1, 1


def kernel_body(
    sizes, block, chunks,
    pos_in, feat_in, charge_in, valid_in, waves_ref, kern_ref, wfeat_ref, wch_ref, wcf_ref,
    bias_ref, wmh_ref, wmf_ref,
    pos_out, charge_out, feat_out, field_out,
    halo, bt_ref, a_ref, msg_ref, yz_ref, w_ref, payload, rs_buf, part_buf, gx_buf, full,
    halo_send, halo_recv, rs_send, rs_recv, gx_send, gx_recv, ag_send, ag_recv,
):
    nx, ny, nz = sizes
    sx, sy, sz = block
    atoms = sx * sy * sz * CAP
    plane = ny * nz
    mx, my, mz = lax.axis_index("gx"), lax.axis_index("gy"), lax.axis_index("gz")
    mp = my * nz + mz
    scale = 1.0 / math.sqrt(nx * sx * ny * sy * nz * sz * CAP * waves_ref.shape[1])

    def plane_id(d):
        p = lax.rem(mp + d, plane)
        return (mx, lax.div(p, nz), lax.rem(p, nz)), p

    barrier = pltpu.get_barrier_semaphore()
    for ddx in range(nx):
        for d in range(plane):
            if ddx == 0 and d == 0:
                continue
            (_, py, pz), _ = plane_id(d)
            pl.semaphore_signal(
                barrier, inc=1, device_id=(lax.rem(mx + ddx, nx), py, pz), device_id_type=MESH
            )

    valid = valid_in[...]
    cell = lax.broadcasted_iota(jnp.int32, (1, atoms), 1) // CAP
    loc = [cell // (sy * sz), (cell // sz) % sy, cell % sz]
    mine = [mx, my, mz]
    side = [nx * sx, ny * sy, nz * sz]
    cell_f = [
        (loc[j] + mine[j] * block[j]).astype(jnp.float32) for j in range(3)
    ]
    local_f = jnp.concatenate([v.astype(jnp.float32) for v in loc], axis=0) - 1.0
    lane = lax.broadcasted_iota(jnp.int32, (8, 128), 1)
    sub = lax.broadcasted_iota(jnp.int32, (8, 128), 0)
    k8 = (lax.broadcasted_iota(jnp.int32, (8, 1), 0) + 1).astype(jnp.float32)

    wy, wz = waves_ref[1:2, :], waves_ref[2:3, :]
    sgy = jnp.where(wy > 0, 1.0, 0.0) - jnp.where(wy < 0, 1.0, 0.0)
    sgz = jnp.where(wz > 0, 1.0, 0.0) - jnp.where(wz < 0, 1.0, 0.0)
    k8i = lax.broadcasted_iota(jnp.int32, (8, 1), 0) + 1
    oz = (jnp.abs(wz) == k8i).astype(jnp.float32)
    oy = (jnp.abs(wy) == k8i).astype(jnp.float32)
    oz0 = (wz == 0).astype(jnp.float32)
    oy0 = (wy == 0).astype(jnp.float32)
    hot = [oy[i : i + 1] * oz for i in range(8)] + [oy0 * oz, oy * oz0, oy0 * oz0 * (k8 == 1.0)]
    kern = kern_ref[...]
    lanes_k = [jnp.where(waves_ref[0:1, :] == i + 1, kern, 0.0) for i in range(8)]
    lanes_k = jnp.concatenate(lanes_k + lanes_k, axis=0)
    kh, kl = split2(lanes_k)
    sx_lane = jnp.where(lane >= 64, 1.0, -1.0)
    hot = jnp.concatenate(hot, axis=0)
    for i, sg in enumerate((None, sgy * sgz, sgy, sgz)):
        oh = (hot if sg is None else hot * sg).astype(jnp.bfloat16)
        w = (dot(oh, kh, NT) + dot(oh, kl, NT)) * scale
        if i >= 2:
            w = w * sx_lane[0:1]
        w_ref[i] = w

    pl.semaphore_wait(barrier, nx * plane - 1)

    def send_halo(step, pos, feats):
        hi, mid, low = split3(pos)
        rec = jnp.concatenate(
            [feats.astype(jnp.float32)]
            + [v.astype(jnp.float32) for v in (hi, mid, low)]
            + [valid, jnp.zeros((REC - 26, atoms), jnp.float32)],
            axis=0,
        ).astype(jnp.bfloat16)
        for x in range(sx):
            for y in range(sy):
                for z in range(sz):
                    n = (x * sy + y) * sz + z
                    halo[step, 1 + x, 1 + y, 1 + z] = rec[:, n * CAP : (n + 1) * CAP]
        copies = []
        for dx in (-1, 0, 1):
            for dy in (-1, 0, 1):
                for dz in (-1, 0, 1):
                    if dx == dy == dz == 0:
                        continue
                    n = len(copies)
                    x, y, z = spans(sx, dx), spans(sy, dy), spans(sz, dz)
                    copy = pltpu.make_async_remote_copy(
                        src_ref=halo.at[
                            step, pl.ds(x[0], x[2]), pl.ds(y[0], y[2]), pl.ds(z[0], z[2])
                        ],
                        dst_ref=halo.at[
                            step, pl.ds(x[1], x[2]), pl.ds(y[1], y[2]), pl.ds(z[1], z[2])
                        ],
                        send_sem=halo_send.at[step, n],
                        recv_sem=halo_recv.at[step, n],
                        device_id=(
                            lax.rem(mx + nx + dx, nx),
                            lax.rem(my + ny + dy, ny),
                            lax.rem(mz + nz + dz, nz),
                        ),
                        device_id_type=MESH,
                    )
                    copy.start()
                    copies.append(copy)
        return copies

    def pair_rows(p, ok, own):
        width = p.shape[1]
        sq = -EXP_COEF * (p[0:1] * p[0:1] + p[1:2] * p[1:2] + p[2:3] * p[2:3])
        one = jnp.ones((3, width), jnp.float32)
        f32 = lambda parts: [v.astype(jnp.float32) for v in parts]
        if own:
            hi, mid, low = f32(split3(p * (2.0 * EXP_COEF)))
            rows = [hi, mid, low, hi, mid, hi, one] + f32(split3(sq))
        else:
            hi, mid, low = f32(split3(p))
            rows = [hi, hi, hi, mid, mid, low] + f32(split3(sq - FAR * (1.0 - ok))) + [one]
        return jnp.concatenate(rows + [jnp.zeros((8, width), jnp.float32)], axis=0)

    def pair_prepare(step, pos):
        own = pair_rows(pos + local_f, None, True).astype(jnp.bfloat16)
        for i in range(sx * sy):
            a_ref[i] = own[:, i * sz * CAP : (i + 1) * sz * CAP]
        wide = (sz + 2) * CAP
        zrow = (lax.broadcasted_iota(jnp.int32, (1, wide), 1) // CAP).astype(jnp.float32) - 2.0

        def prepare(g, carry):
            gx_i, gy_i = lax.div(g, sy + 2), lax.rem(g, sy + 2)
            rec = jnp.concatenate(
                [halo[step, gx_i, gy_i, z] for z in range(sz + 2)], axis=1
            ).astype(jnp.float32)
            p = rec[16:19] + rec[19:22] + rec[22:25]
            ones = jnp.ones((1, wide), jnp.float32)
            base = jnp.concatenate(
                [
                    ones * (gx_i.astype(jnp.float32) - 2.0),
                    ones * (gy_i.astype(jnp.float32) - 2.0),
                    zrow,
                ],
                axis=0,
            )
            bt_ref[g] = jnp.transpose(pair_rows(p + base, rec[25:26], False)).astype(jnp.bfloat16)
            return carry

        lax.fori_loop(0, (sx + 2) * (sy + 2), prepare, 0)

    def pair_columns(step, first, last):
        def per_column(i, carry):
            x, y = lax.div(i, sy), lax.rem(i, sy)
            for z in range(sz):
                mine_a = a_ref[i, :, z * CAP : (z + 1) * CAP]
                total = jnp.zeros((REC, CAP), jnp.float32)
                for dx in range(3):
                    for dy in range(3):
                        g = (x + dx) * (sy + 2) + y + dy
                        rows = bt_ref[g, z * CAP : (z + 3) * CAP, :]
                        weight = jnp.exp2(dot(rows, mine_a, NN)).astype(jnp.bfloat16)
                        rec = jnp.concatenate(
                            [halo[step, x + dx, y + dy, z + k] for k in range(3)], axis=1
                        )
                        total = total + dot(rec, weight, NN)
                msg_ref[i, :, z * CAP : (z + 1) * CAP] = total
            return carry

        lax.fori_loop(first, last, per_column, 0)

    def pair_finish():
        total = jnp.concatenate([msg_ref[i] for i in range(sx * sy)], axis=1) * valid
        return total[0:16] / jnp.sqrt(jnp.maximum(total[25:26], 1.0))

    def sum_scatter(r):
        rows = chunks[r % ITERS]
        copies = []
        for d in range(1, plane):
            device, p = plane_id(d)
            copy = pltpu.make_async_remote_copy(
                src_ref=payload.at[r, pl.ds(pl.multiple_of(p * rows, 8), rows)],
                dst_ref=rs_buf.at[r, d, pl.ds(0, rows)],
                send_sem=rs_send.at[r, d],
                recv_sem=rs_recv.at[r, d],
                device_id=device,
                device_id_type=MESH,
            )
            copy.start()
            copies.append(copy)
        return copies

    def sum_across(r, copies):
        rows = chunks[r % ITERS]
        total = payload[r, pl.ds(pl.multiple_of(mp * rows, 8), rows)]
        for d in range(1, plane):
            copies[d - 1].wait_recv()
            total = total + rs_buf[r, d, 0:rows]
        part_buf[r, 0, 0:rows] = total
        copies_x = []
        for d in range(1, nx):
            copy = pltpu.make_async_remote_copy(
                src_ref=part_buf.at[r, 0, pl.ds(0, rows)],
                dst_ref=gx_buf.at[r, d, pl.ds(0, rows)],
                send_sem=gx_send.at[r, d],
                recv_sem=gx_recv.at[r, d],
                device_id=(lax.rem(mx + d, nx), my, mz),
                device_id_type=MESH,
            )
            copy.start()
            copies_x.append(copy)
        return copies_x

    def sum_gather(r, copies_x):
        rows = chunks[r % ITERS]
        total = part_buf[r, 0, 0:rows]
        for d in range(1, nx):
            copies_x[d - 1].wait_recv()
            total = total + gx_buf[r, d, 0:rows]
        here = pl.ds(pl.multiple_of(mp * rows, 8), rows)
        full[r, here] = total
        copies_g = []
        for d in range(1, plane):
            device, _ = plane_id(d)
            copy = pltpu.make_async_remote_copy(
                src_ref=full.at[r, here],
                dst_ref=full.at[r, here],
                send_sem=ag_send.at[r, d],
                recv_sem=ag_recv.at[r, d],
                device_id=device,
                device_id_type=MESH,
            )
            copy.start()
            copies_g.append(copy)
        return copies_g

    def sum_end(copies, copies_x, copies_g):
        for copy in copies_g:
            copy.wait_recv()
        for copy in copies + copies_x + copies_g:
            copy.wait_send()

    def sum_payload(r, charge):
        qx = jnp.concatenate([x * charge for x in xs], axis=0)
        qh, ql = split2(qx)
        payload[r, 0 : N_P * 8] = dot(yh, qh, NT) + (dot(yh, ql, NT) + dot(yl, qh, NT))
        col = jnp.sum(charge, axis=1, keepdims=True)
        totals = jnp.sum(jnp.where(lane % 8 == sub, col, 0.0), axis=0, keepdims=True)
        payload[r, TOT * 8 : TOT * 8 + 8] = jnp.where(sub == 0, totals, count_row)
        used = (TILES if r % ITERS == 0 else PV0) * 8
        if plane * chunks[r % ITERS] > used:
            payload[r, used : plane * chunks[r % ITERS]] = jnp.zeros(
                (plane * chunks[r % ITERS] - used, 128), jnp.float32
            )

    def trig(pos):
        out = []
        for j in range(3):
            u = (cell_f[j] + pos[j : j + 1]) / float(side[j])
            t = k8 * u
            t = t - jnp.floor(t + 0.5)
            s = t * t
            out.append((horner(COS_POLY, s), t * horner(SIN_POLY, s)))
        return out

    block_ones = (
        lax.broadcasted_iota(jnp.int32, (128, 128), 0) // 8
        == lax.broadcasted_iota(jnp.int32, (128, 128), 1) // 8
    ).astype(jnp.bfloat16)

    pos = pos_in[...]
    feats = feat_in[...]
    charge = charge_in[...] * valid
    field = None
    count_row = jnp.zeros((1, 128), jnp.float32) + jnp.sum(valid, axis=1, keepdims=True)
    for step in range(STEPS):
        copies = send_halo(step, pos, feats)
        (cx, sxn), (cy, syn), (cz, szn) = trig(pos)
        xs = [v[i : i + 1] for v in (cx, sxn) for i in range(8)]
        zz = jnp.concatenate([cz, szn], axis=0)
        for i in range(16):
            yrow = (cy, syn)[i // 8][i % 8 : i % 8 + 1]
            yz_ref[i * 16 : (i + 1) * 16, :] = yrow * zz
        yz_ref[256:272, :] = zz
        yz_ref[272:288, :] = jnp.concatenate([cy, syn], axis=0)
        yz_ref[288:296, :] = jnp.where(k8 == 1.0, 1.0, 0.0) * jnp.ones((8, atoms), jnp.float32)
        yz = yz_ref[...]
        yh, yl = split2(yz)
        valid8 = jnp.ones((8, 1), jnp.float32) * valid
        xv = jnp.concatenate([x * valid8 for x in xs], axis=0)
        vh, vl = split2(xv)
        pv = dot(yh, vh, NT) + (dot(yh, vl, NT) + dot(yl, vh, NT))
        for t in range(TILES_PV):
            packed = jnp.zeros((8, 128), jnp.float32)
            for g in range(8):
                if t * 8 + g < N_P:
                    n = t * 8 + g
                    packed = jnp.where(lane % 8 == g, pv[n * 8 : n * 8 + 8], packed)
            payload[step * ITERS, (PV0 + t) * 8 : (PV0 + t + 1) * 8] = packed
        first = step * ITERS
        sum_payload(first, charge)
        started = sum_scatter(first)
        crossed = sum_across(first, started)
        for copy in copies:
            copy.wait()
        pair_prepare(step, pos)
        half = sx * sy // 2
        pair_columns(step, 0, half)
        gathered = sum_gather(first, crossed)
        pair_columns(step, half, sx * sy)
        message = pair_finish()
        feats = (
            feats.astype(jnp.float32)
            + jnp.tanh(dot(wfeat_ref[...], message, TN, HI))
        ).astype(jnp.bfloat16)
        hproj = dot(wch_ref[...], feats.astype(jnp.float32), TN, HI) + bias_ref[...]
        for sweep in range(ITERS):
            r = step * ITERS + sweep
            if sweep > 0:
                sum_payload(r, charge)
                started = sum_scatter(r)
                crossed = sum_across(r, started)
                gathered = sum_gather(r, crossed)
            sum_end(started, crossed, gathered)
            if sweep == 0:
                spread = []
                for n in range(N_P):
                    packed = full[r, (PV0 + n // 8) * 8 : (PV0 + n // 8) * 8 + 8]
                    spread.append(jnp.where(lane % 8 == n % 8, packed, 0.0))
                sh, sm, sl = split3(jnp.concatenate(spread, axis=0))
                pv_all = dot(sh, block_ones, NN) + dot(sm, block_ones, NN) + dot(sl, block_ones, NN)
            tot = full[r, TOT * 8 : TOT * 8 + 8]
            mean_row = tot[0:1] / tot[1:2]
            mean_col = jnp.sum(
                jnp.where(lane == sub, jnp.broadcast_to(mean_row, (8, 128)), 0.0),
                axis=1, keepdims=True,
            )
            neutral = valid * (charge - mean_col)
            p_all = full[r, 0 : N_P * 8] - mean_row * pv_all
            p_roll = pltpu.roll(p_all, 64, 1)
            tile = lambda a, n: a[n * 8 : n * 8 + 8]
            t_rows = []
            for yr in range(2):
                for ky in range(8):
                    for zr in range(2):
                        w = [w_ref[i, ky * 8 : ky * 8 + 8] for i in range(4)]
                        at = lambda a, b: ((a * 8 + ky) * 2 + b)
                        s_y, s_z = 2.0 * yr - 1.0, 2.0 * zr - 1.0
                        t_rows.append(
                            w[0] * tile(p_all, at(yr, zr))
                            - (s_y * s_z) * w[1] * tile(p_all, at(1 - yr, 1 - zr))
                            - s_y * w[2] * tile(p_roll, at(1 - yr, zr))
                            - s_z * w[3] * tile(p_roll, at(yr, 1 - zr))
                        )
            for zr in range(2):
                t_rows.append(
                    w_ref[0, 64:72] * tile(p_all, 32 + zr)
                    - (2.0 * zr - 1.0) * w_ref[3, 64:72] * tile(p_roll, 32 + 1 - zr)
                )
            for yr in range(2):
                t_rows.append(
                    w_ref[0, 72:80] * tile(p_all, 34 + yr)
                    - (2.0 * yr - 1.0) * w_ref[2, 72:80] * tile(p_roll, 34 + 1 - yr)
                )
            t_rows.append(w_ref[0, 80:88] * tile(p_all, 36))
            t_all = jnp.transpose(jnp.concatenate(t_rows, axis=0))
            fh, fl = split2(t_all)
            f_all = dot(fh, yh, NN) + (dot(fh, yl, NN) + dot(fl, yh, NN))
            field = xs[0] * f_all[0:8]
            for i in range(1, 16):
                field = field + xs[i] * f_all[i * 8 : i * 8 + 8]
            fproj = dot(wcf_ref[...], field, TN, HI)
            charge = valid * (0.5 * neutral + jnp.tanh(hproj + fproj))
        move = jnp.tanh(
            dot(wmh_ref[...], message, TN, HI) + dot(wmf_ref[...], field, TN, HI)
        )
        pos = pos + STEP_LEN * valid * move
    pos_out[...] = pos
    charge_out[...] = charge
    feat_out[...] = feats
    field_out[...] = field


def on_device(
    sizes, offsets, features, charges, counts, waves, kernel,
    w_feat, w_charge_h, w_charge_f, charge_bias, w_move_h, w_move_f,
):
    nx, ny, nz = sizes
    block = offsets.shape[1:4]
    sx, sy, sz = block
    atoms = sx * sy * sz * CAP
    plane = ny * nz
    chunk = -(-TILES // plane) * 8
    chunks = (chunk,) + (-(-PV0 // plane) * 8,) * (ITERS - 1)
    rounds = STEPS * ITERS
    valid = (jnp.arange(CAP, dtype=jnp.int32) < counts[..., None]).astype(jnp.float32)
    args = (
        offsets.reshape(3, atoms), features.reshape(16, atoms), charges.reshape(8, atoms),
        valid.reshape(1, atoms), waves, kernel, w_feat, w_charge_h, w_charge_f,
        charge_bias.reshape(8, 1), w_move_h, w_move_f,
    )
    vmem = pl.BlockSpec(memory_space=pltpu.VMEM)
    dma = pltpu.SemaphoreType.DMA
    outs = pl.pallas_call(
        functools.partial(kernel_body, sizes, block, chunks),
        out_shape=(
            jax.ShapeDtypeStruct((3, atoms), jnp.float32),
            jax.ShapeDtypeStruct((8, atoms), jnp.float32),
            jax.ShapeDtypeStruct((16, atoms), jnp.bfloat16),
            jax.ShapeDtypeStruct((8, atoms), jnp.float32),
        ),
        in_specs=[vmem] * len(args),
        out_specs=(vmem,) * 4,
        scratch_shapes=[
            pltpu.VMEM((STEPS, sx + 2, sy + 2, sz + 2, REC, CAP), jnp.bfloat16),
            pltpu.VMEM(((sx + 2) * (sy + 2), (sz + 2) * CAP, 32), jnp.bfloat16),
            pltpu.VMEM((sx * sy, 32, sz * CAP), jnp.bfloat16),
            pltpu.VMEM((sx * sy, REC, sz * CAP), jnp.float32),
            pltpu.VMEM((N_P * 8, atoms), jnp.float32),
            pltpu.VMEM((4, 88, 128), jnp.float32),
            pltpu.VMEM((rounds, plane * chunk, 128), jnp.float32),
            pltpu.VMEM((rounds, plane, chunk, 128), jnp.float32),
            pltpu.VMEM((rounds, 1, chunk, 128), jnp.float32),
            pltpu.VMEM((rounds, nx, chunk, 128), jnp.float32),
            pltpu.VMEM((rounds, plane * chunk, 128), jnp.float32),
            dma((STEPS, 26)), dma((STEPS, 26)),
            dma((rounds, plane)), dma((rounds, plane)),
            dma((rounds, nx)), dma((rounds, nx)),
            dma((rounds, plane)), dma((rounds, plane)),
        ],
        compiler_params=pltpu.CompilerParams(
            collective_id=0, has_side_effects=True, vmem_limit_bytes=48 * 1024 * 1024
        ),
    )(*args)
    return (
        outs[0].reshape(offsets.shape), outs[1].reshape(charges.shape),
        outs[2].reshape(features.shape), outs[3].reshape(charges.shape),
    )


def solution(mesh):
    grid = P(None, "gx", "gy", "gz", None)
    sizes = tuple(mesh.shape[a] for a in ("gx", "gy", "gz"))
    return jax.shard_map(
        functools.partial(on_device, sizes),
        mesh=mesh,
        in_specs=(grid, grid, grid, P("gx", "gy", "gz")) + (P(),) * 8,
        out_specs=(grid,) * 4,
        check_vma=False,
    )
```
